256 devices in a mesh: src: 32 (over y, x, z_hi), tgt: 8 (over z_lo, core).
Axes of the slice: x: 4, y: 4, z: 8 (z_hi: 2, z_lo: 4; z = z_hi * 4 + z_lo), core: 2. Of those that a mesh axis runs over, the one named last changes fastest.
Arguments:
- source_bands: bfloat16 [32, 128, 128, 128], P('src', 'tgt'), may hold values from -6 to 6
- target_bands: bfloat16 [8, 128, 128, 128], P('tgt', 'src'), may hold values from -6 to 6
Outputs:
- exchange_field: float32 [8, 128, 128, 128], P('tgt', 'src')
The draws below stay inside these ranges and needn't reach their ends.
All inputs are finite; a program needn't handle non-finite values.
Results may differ from the reference program's by a relative error of at most 0.033.
Values may be sent and summed in bfloat16 or wider, within the bound.
No kernel may reach another device: no remote copies, remote signals or barrier semaphores. Data moves between devices by JAX's collectives and lax.ppermute only.
A program may use at most 128 MiB of HBM per device.

```python
import math
import jax
import jax.numpy as jnp
from jax import lax

NX = 128
NY = 128
NZ = 128
SRC_DEV = 1
SRC_BANDS = 32
TGT_BANDS = 8
N_SRC = 32


def shard_levels(own_key, shape, cuts, low, high):
    loudness = 1.0
    for axis_at, shards_of in cuts:
        heights = jax.random.uniform(jax.random.fold_in(jax.random.fold_in(own_key, 6), axis_at), (shards_of,), jnp.float32, low / len(cuts), high / len(cuts))
        loudness = loudness * jnp.repeat(jnp.exp(heights), shape[axis_at] // shards_of).reshape((-1,) + (1,) * (len(shape) - 1 - axis_at))
    return loudness


def bell_draw(rng, dims, width, limit, split=(), held_as=jnp.bfloat16):
    loudness = shard_levels(rng, dims, split, -0.22, 0.18) if split else 1.0
    values = jax.random.normal(rng, dims, jnp.float32) * width * loudness
    return jnp.minimum(jnp.maximum(values, -limit), limit).astype(held_as)


def setup_inputs(seed: int = 0) -> dict:
    key_of = jax.random.split(jax.random.key(seed), 3)
    source_bands = bell_draw(key_of[0], (SRC_BANDS, NX, NY, NZ), 1.0, 6.0, ((0, 32), (1, 8)))
    target_bands = bell_draw(key_of[1], (TGT_BANDS, NX, NY, NZ), 1.0, 6.0, ((0, 8), (1, 32)))
    return {"source_bands": source_bands, "target_bands": target_bands}


FRACTION = 0.25
CELL = 59.2
ALONG_Z = '...xyz,zk->...xyk'
ALONG_Y = '...xyz,yk->...xkz'
ALONG_X = '...xyz,xk->...kyz'

def tables(points):
    counter = jnp.arange(points, dtype=jnp.int32)
    product = counter[:, None] * counter[None, :] % points
    angles = 2.0 * math.pi / points * product.astype(jnp.float32)
    return (jnp.cos(angles).astype(jnp.bfloat16), jnp.sin(angles).astype(jnp.bfloat16))

def wave_squares(points):
    counter = jnp.arange(points, dtype=jnp.int32)
    wrapped = jnp.where(counter < points // 2, counter, counter - points)
    frequency = 2.0 * math.pi / CELL * wrapped.astype(jnp.float32)
    return frequency * frequency

def coulomb_kernel():
    wave_sq = wave_squares(NX)[:, None, None] + wave_squares(NY)[None, :, None] + wave_squares(NZ)[None, None, :]
    radius = CELL * (3.0 / (4.0 * math.pi)) ** (1.0 / 3.0)
    safe_sq = jnp.where(wave_sq > 0, wave_sq, 1.0)
    magnitude = jnp.sqrt(safe_sq)
    values = jnp.where(wave_sq > 0, 4.0 * math.pi * (1.0 - jnp.cos(magnitude * radius)) / safe_sq, 2.0 * math.pi * radius * radius)
    return values / (NX * NY * NZ)

def contract(operand, table, pattern):
    return jnp.einsum(pattern, operand.astype(jnp.float32), table.astype(jnp.float32))

def rotate(real_part, imag_part, cos_table, sin_table, pattern, direction):
    new_real = contract(real_part, cos_table, pattern) + direction * contract(imag_part, sin_table, pattern)
    new_imag = contract(imag_part, cos_table, pattern) - direction * contract(real_part, sin_table, pattern)
    return (new_real.astype(jnp.bfloat16), new_imag.astype(jnp.bfloat16))

def reference(source_bands, target_bands):
    kernel = coulomb_kernel()
    cos_x, sin_x = tables(NX)
    cos_y, sin_y = tables(NY)
    cos_z, sin_z = tables(NZ)
    grouped = source_bands.reshape((N_SRC, SRC_DEV, NX, NY, NZ))

    def one_target(target):

        def add_source(running, source):
            density = (source.astype(jnp.float32) * target.astype(jnp.float32)).astype(jnp.bfloat16)
            real_part = contract(density, cos_z, ALONG_Z).astype(jnp.bfloat16)
            imag_part = (-contract(density, sin_z, ALONG_Z)).astype(jnp.bfloat16)
            real_part, imag_part = rotate(real_part, imag_part, cos_y, sin_y, ALONG_Y, 1.0)
            real_part, imag_part = rotate(real_part, imag_part, cos_x, sin_x, ALONG_X, 1.0)
            real_part = (real_part.astype(jnp.float32) * kernel).astype(jnp.bfloat16)
            imag_part = (imag_part.astype(jnp.float32) * kernel).astype(jnp.bfloat16)
            real_part, imag_part = rotate(real_part, imag_part, cos_z, sin_z, ALONG_Z, -1.0)
            real_part, imag_part = rotate(real_part, imag_part, cos_y, sin_y, ALONG_Y, -1.0)
            potential = contract(real_part, cos_x, ALONG_X) - contract(imag_part, sin_x, ALONG_X)
            return (running + source.astype(jnp.float32) * potential, None)

        def add_group(total, group):
            inner, _ = lax.scan(add_source, jnp.zeros((NX, NY, NZ), jnp.float32), group)
            rounded = lax.optimization_barrier((-FRACTION * inner).astype(jnp.bfloat16))
            return (total + rounded.astype(jnp.float32), None)
        total, _ = lax.scan(add_group, jnp.zeros((NX, NY, NZ), jnp.float32), grouped)
        return total
    return lax.map(one_target, target_bands)
```

```python
import functools
import math

import jax
import jax.numpy as jnp
import ml_dtypes
import numpy as np
from jax import lax
from jax.experimental import pallas as pl
from jax.experimental.pallas import tpu as pltpu
from jax.sharding import Mesh
from jax.sharding import PartitionSpec as P

N = 128
HALF = N // 2
KEPT = HALF + 1
SLAB = 16
PLANES = KEPT + 1
CHUNK = 13
FRACTION = 0.25
CELL = 59.2
BF16 = jnp.bfloat16
F32 = jnp.float32


def tables():
    counter = np.arange(N)
    angles = (2.0 * math.pi / N) * (counter[:, None] * counter[None, :] % N)
    cos = np.cos(angles)
    sin = np.sin(angles)
    first = np.concatenate([cos[:KEPT], -sin[1:HALF]], axis=0)
    weight = np.full(N, 2.0)
    weight[0] = weight[HALF] = 1.0
    last = -FRACTION * np.concatenate(
        [cos[:, :KEPT] * weight[None, :KEPT], -2.0 * sin[:, 1:HALF]], axis=1
    )
    forward = np.block([[cos, -sin], [sin, cos]])
    inverse = np.block([[cos, sin], [-sin, cos]])
    every = (first, last, forward, inverse, forward.T, inverse.T)
    return [np.asarray(t, np.float32).astype(ml_dtypes.bfloat16) for t in every]


def coulomb_kernel():
    counter = np.arange(N)
    wrapped = np.where(counter < HALF, counter, counter - N)
    wave = (2.0 * math.pi / CELL * wrapped) ** 2
    wave_sq = wave[:KEPT, None, None] + wave[None, :, None] + wave[None, None, :]
    radius = CELL * (3.0 / (4.0 * math.pi)) ** (1.0 / 3.0)
    safe_sq = np.where(wave_sq > 0, wave_sq, 1.0)
    values = np.where(
        wave_sq > 0,
        4.0 * math.pi * (1.0 - np.cos(np.sqrt(safe_sq) * radius)) / safe_sq,
        2.0 * math.pi * radius * radius,
    )
    values = values / N**3
    return np.concatenate([values, np.zeros((1, N, N))]).astype(np.float32)


def dot(left, right):
    return jnp.dot(left, right, preferred_element_type=F32)


def pair_kernel(
    core_ref, s_ring, s_other, t_mine, t_other, kernel_hbm,
    first, last, lane_fwd, lane_inv, row_fwd, row_inv,
    keep, give,
    s_buf, t_buf, k_buf, spec, wide, pq, in_sem, k_sem, out_sem,
):
    core = core_ref[0]
    other = 1 - core

    def loads(part):
        four = pl.ds(4 * part, 4)
        return (
            pltpu.make_async_copy(s_ring.at[core, part], s_buf.at[part, core], in_sem.at[part, 0]),
            pltpu.make_async_copy(s_other.at[part], s_buf.at[part, other], in_sem.at[part, 1]),
            pltpu.make_async_copy(t_mine.at[four], t_buf.at[four, core], in_sem.at[part, 2]),
            pltpu.make_async_copy(t_other.at[four], t_buf.at[four, other], in_sem.at[part, 3]),
        )

    def stores(part):
        four = pl.ds(4 * part, 4)
        return (
            pltpu.make_async_copy(t_buf.at[four, core], keep.at[four], out_sem.at[part, 0]),
            pltpu.make_async_copy(t_buf.at[four, other], give.at[four], out_sem.at[part, 1]),
        )

    for part in range(4):
        for copy in loads(part):
            copy.start()
    k_copy = pltpu.make_async_copy(kernel_hbm, k_buf, k_sem)
    k_copy.start()

    spec[KEPT] = jnp.zeros((2 * N, N), BF16)
    pq[0:SLAB, N:] = jnp.zeros((SLAB, N), BF16)
    pq[HALF * SLAB :, N:] = jnp.zeros((SLAB, N), BF16)

    def t_at(slab, j):
        return (2 * slab + j // 8, (j // 4) % 2, j % 4)

    def forward_slab(slab, _):
        part = slab // 2
        half = slab % 2

        @pl.when(half == 0)
        def _():
            for copy in loads(part):
                copy.wait()

        for j in range(0, SLAB, 2):
            density = jnp.concatenate(
                [s_buf[part, half, j + i] * t_buf[t_at(slab, j + i)] for i in range(2)], axis=1
            )
            out = dot(first[...], density)
            wide[pl.ds(j * N, N)] = out[:, :N]
            wide[pl.ds((j + 1) * N, N)] = out[:, N:]
        for k in range(KEPT):
            rows = pl.ds(k * SLAB, SLAB)
            pq[rows, 0:N] = wide[pl.ds(k, SLAB, stride=N)].astype(BF16)
            if 0 < k < HALF:
                pq[rows, N:] = wide[pl.ds(HALF + k, SLAB, stride=N)].astype(BF16)
        at = pl.multiple_of(slab * SLAB, SLAB)
        for i in range(KEPT // CHUNK):
            out = dot(pq[pl.ds(i * CHUNK * SLAB, CHUNK * SLAB)], lane_fwd[...]).astype(BF16)
            ks = pl.ds(i * CHUNK, CHUNK)
            spec[ks, pl.ds(at, SLAB)] = out[:, :N].reshape(CHUNK, SLAB, N)
            spec[ks, pl.ds(N + at, SLAB)] = out[:, N:].reshape(CHUNK, SLAB, N)
        return 0

    lax.fori_loop(0, N // SLAB, forward_slab, 0)
    k_copy.wait()

    def middle(step, _):
        for u in range(3):
            k = step * 6 + 2 * u
            both = jnp.concatenate([spec[k], spec[k + 1]], axis=1)
            out = dot(row_fwd[...], both)
            scale = jnp.concatenate([k_buf[k], k_buf[k + 1]], axis=1)
            out = jnp.concatenate([out[:N] * scale, out[N:] * scale], axis=0).astype(BF16)
            out = dot(row_inv[...], out).astype(BF16)
            spec[k] = out[:, :N]
            spec[k + 1] = out[:, N:]
        return 0

    lax.fori_loop(0, PLANES // 6, middle, 0)

    def inverse_slab(slab, _):
        part = slab // 2
        half = slab % 2
        at = pl.multiple_of(slab * SLAB, SLAB)
        for i in range(KEPT // CHUNK):
            ks = pl.ds(i * CHUNK, CHUNK)
            p = spec[ks, pl.ds(at, SLAB)].reshape(CHUNK * SLAB, N)
            q = spec[ks, pl.ds(N + at, SLAB)].reshape(CHUNK * SLAB, N)
            out = dot(jnp.concatenate([p, q], axis=1), lane_inv[...])
            wide[pl.ds(i * CHUNK * SLAB, CHUNK * SLAB)] = out[:, :N]
            lo = max(i * CHUNK, 1)
            hi = min((i + 1) * CHUNK, HALF)
            base = i * CHUNK
            wide[pl.ds((HALF + lo) * SLAB, (hi - lo) * SLAB)] = out[
                (lo - base) * SLAB : (hi - base) * SLAB, N:
            ]
        for j in range(0, SLAB, 2):
            half_spec = jnp.concatenate(
                [wide[pl.ds(j + i, N, stride=SLAB)].astype(BF16) for i in range(2)], axis=1
            )
            out = dot(last[...], half_spec)
            for i in range(2):
                term = out[:, i * N : (i + 1) * N] * s_buf[part, half, j + i].astype(F32)
                t_buf[t_at(slab, j + i)] = term.astype(BF16)

        @pl.when(half == 1)
        def _():
            for copy in stores(part):
                copy.start()

        return 0

    lax.fori_loop(0, N // SLAB, inverse_slab, 0)
    for part in range(4):
        for copy in stores(part):
            copy.wait()


ANY = pl.BlockSpec(memory_space=pl.ANY)
VMEM = pl.BlockSpec(memory_space=pltpu.VMEM)
SMEM = pl.BlockSpec(memory_space=pltpu.SMEM)


def exchange_pair(core, s_ring, s_other, t_mine, t_other):
    half = jax.ShapeDtypeStruct((16, 4, N, N), BF16)
    consts = [jnp.asarray(t) for t in tables()]
    return pl.pallas_call(
        pair_kernel,
        out_shape=(half, half),
        in_specs=[SMEM] + [ANY] * 5 + [VMEM] * 6,
        out_specs=(ANY, ANY),
        scratch_shapes=[
            pltpu.VMEM((4, 2, SLAB, N, N), BF16),
            pltpu.VMEM((16, 2, 4, N, N), BF16),
            pltpu.VMEM((PLANES, N, N), F32),
            pltpu.VMEM((PLANES, 2 * N, N), BF16),
            pltpu.VMEM((SLAB * N, N), F32),
            pltpu.VMEM((KEPT * SLAB, 2 * N), BF16),
            pltpu.SemaphoreType.DMA((4, 4)),
            pltpu.SemaphoreType.DMA,
            pltpu.SemaphoreType.DMA((4, 2)),
        ],
        compiler_params=pltpu.CompilerParams(vmem_limit_bytes=40 * 1024 * 1024),
        cost_estimate=pl.CostEstimate(
            flops=2 * 42000 * 256 * 256, bytes_accessed=17 << 20, transcendentals=0
        ),
        name="exchange_pair",
    )(core, s_ring, s_other, t_mine, t_other, jnp.asarray(coulomb_kernel()), *consts)


def split_kernel(place, mine, theirs, *refs):
    outs, (a_buf, b_buf, in_sem, out_sem) = refs[:8], refs[8:]
    y, x = place[0], place[1]
    loads = []
    for i in range(4):
        four = pl.ds(4 * i, 4)
        loads.append(pltpu.make_async_copy(mine.at[four], a_buf.at[i], in_sem.at[i, 0]))
        loads.append(pltpu.make_async_copy(theirs.at[four], b_buf.at[i], in_sem.at[i, 1]))
    for copy in loads:
        copy.start()
    for i in range(4):
        loads[2 * i].wait()
        loads[2 * i + 1].wait()

        def add(j, _):
            total = a_buf[i, j].astype(F32) + b_buf[i, j].astype(F32)
            a_buf[i, j] = total.astype(BF16)
            return 0

        lax.fori_loop(0, 4, add, 0)
    copies = []
    for d in range(4):
        to_x = lax.rem(x + d, 4)
        to_y = lax.rem(y + d, 4)
        copies.append(
            pltpu.make_async_copy(a_buf.at[:, to_x, 0:2], outs[d], out_sem.at[d, 0])
        )
        copies.append(
            pltpu.make_async_copy(a_buf.at[to_y, :, 2:4], outs[4 + d], out_sem.at[d, 1])
        )
    for copy in copies:
        copy.start()
    for copy in copies:
        copy.wait()


def split_sum(place, mine, theirs):
    piece = jax.ShapeDtypeStruct((4, 2, N, N), BF16)
    return pl.pallas_call(
        split_kernel,
        out_shape=(piece,) * 8,
        in_specs=[SMEM, ANY, ANY],
        out_specs=(ANY,) * 8,
        scratch_shapes=[
            pltpu.VMEM((4, 4, 4, N, N), BF16),
            pltpu.VMEM((4, 4, 4, N, N), BF16),
            pltpu.SemaphoreType.DMA((4, 2)),
            pltpu.SemaphoreType.DMA((4, 2)),
        ],
        compiler_params=pltpu.CompilerParams(vmem_limit_bytes=16 * 1024 * 1024),
        name="split_sum",
    )(place, mine, theirs)


def shift(value, axis, by):
    return lax.ppermute(value, axis, [(i, (i + by) % 4) for i in range(4)])


def swap_core(value):
    return lax.ppermute(value, "c", [(0, 1), (1, 0)])


def swap_roles(value):
    return lax.ppermute(value, ("h", "c"), [(0, 0), (1, 2), (2, 1), (3, 3)])


def gather_four(value, axis, place):
    got = [value] + [shift(value, axis, d) for d in (1, 2, 3)]
    out = jnp.zeros((4,) + value.shape, value.dtype)
    for d in range(4):
        out = lax.dynamic_update_index_in_dim(out, got[d], lax.rem(place - d + 4, 4), 0)
    return out


def on_device(source_bands, target_bands):
    y, x, core = lax.axis_index("y"), lax.axis_index("x"), lax.axis_index("c")
    s_ring = lax.all_gather(source_bands[0], ("h", "l"), axis=0, tiled=True)
    s_ring = s_ring.reshape(2, 4, SLAB, N, N)
    s_other = swap_core(lax.dynamic_index_in_dim(s_ring, 1 - core, 0, keepdims=False))

    target = swap_roles(target_bands[0])
    by_x = gather_four(gather_four(target[:2], "x", x), "y", y)
    by_y = gather_four(gather_four(target[2:], "y", y), "x", x)
    t_mine = jnp.concatenate([by_x, jnp.swapaxes(by_y, 0, 1)], axis=2).reshape(16, 4, N, N)
    t_other = swap_core(t_mine)

    core_at = core.astype(jnp.int32).reshape(1)
    keep, give = exchange_pair(core_at, s_ring, s_other, t_mine, t_other)
    got = swap_core(give)
    place = jnp.stack([y, x]).astype(jnp.int32)
    pieces = split_sum(place, keep, got)

    def total(parts):
        return functools.reduce(jnp.add, [p.astype(F32) for p in parts])

    def two_stage(own, others, axes, places):
        come = [own] + [shift(o, axes[0], d + 1) for d, o in enumerate(others)]
        part = total(come).astype(BF16)
        back = [
            lax.dynamic_index_in_dim(part, lax.rem(places[1] + d, 4), 0, keepdims=False)
            for d in range(4)
        ]
        come = [back[0]] + [shift(b, axes[1], d + 1) for d, b in enumerate(back[1:])]
        return total(come)

    low = two_stage(pieces[0], pieces[1:4], ("x", "y"), (x, y))
    high = two_stage(pieces[4], pieces[5:8], ("y", "x"), (y, x))
    field = jnp.concatenate([low, high], axis=0).astype(BF16)
    return swap_roles(field).astype(F32)[None]


def solution(mesh):
    fine = Mesh(mesh.devices.reshape(4, 4, 2, 4, 2), ("y", "x", "h", "l", "c"))
    src, tgt = ("y", "x", "h"), ("l", "c")
    return jax.shard_map(
        on_device,
        mesh=fine,
        in_specs=(P(src, tgt, None, None), P(tgt, src, None, None)),
        out_specs=P(tgt, src, None, None),
        check_vma=False,
    )
```

```python
import functools
import math

import jax
import jax.numpy as jnp
import ml_dtypes
import numpy as np
from jax import lax
from jax.experimental import pallas as pl
from jax.experimental.pallas import tpu as pltpu
from jax.sharding import Mesh
from jax.sharding import PartitionSpec as P

N = 128
HALF = N // 2
KEPT = HALF + 1
SLAB = 16
PLANES = KEPT + 1
SHARE = PLANES // 2
CHUNK = 11
FIRST_PITCH = N + 8
LAST_PITCH = SLAB + 8
FRACTION = 0.25
CELL = 59.2
MIB = 1024 * 1024
BF16 = jnp.bfloat16
F32 = jnp.float32


def tables():
    counter = np.arange(N)
    angles = (2.0 * math.pi / N) * (counter[:, None] * counter[None, :] % N)
    cos = np.cos(angles)
    sin = np.sin(angles)
    first = np.concatenate([cos[:KEPT], -sin[1:HALF]], axis=0)
    weight = np.full(N, 2.0)
    weight[0] = weight[HALF] = 1.0
    last = -FRACTION * np.concatenate(
        [cos[:, :KEPT] * weight[None, :KEPT], -2.0 * sin[:, 1:HALF]], axis=1
    )
    forward = np.block([[cos, -sin], [sin, cos]])
    inverse = np.block([[cos, sin], [-sin, cos]])
    x = np.arange(N).reshape(4, 2, 2, 2, 4)
    order = np.concatenate([x[:, :, :, c][:, [c, 1 - c]].reshape(HALF) for c in range(2)])
    both = np.concatenate([order, order + N])
    every = (first, last, forward, inverse, forward.T[:, both], inverse.T[both, :])
    return [np.asarray(t, np.float32).astype(ml_dtypes.bfloat16) for t in every]


def coulomb_kernel():
    counter = np.arange(N)
    wrapped = np.where(counter < HALF, counter, counter - N)
    wave = (2.0 * math.pi / CELL * wrapped) ** 2
    wave_sq = wave[:KEPT, None, None] + wave[None, :, None] + wave[None, None, :]
    radius = CELL * (3.0 / (4.0 * math.pi)) ** (1.0 / 3.0)
    safe_sq = np.where(wave_sq > 0, wave_sq, 1.0)
    values = np.where(
        wave_sq > 0,
        4.0 * math.pi * (1.0 - np.cos(np.sqrt(safe_sq) * radius)) / safe_sq,
        2.0 * math.pi * radius * radius,
    )
    values = values / N**3
    values = np.concatenate([values, np.zeros((1, N, N))]).astype(np.float32)
    return values.astype(ml_dtypes.bfloat16).reshape(2, SHARE, N, N)


def dot(left, right):
    return jnp.dot(left, right, preferred_element_type=F32)


def forward_kernel(count, info, *refs):
    pieces, t_all, first, lane_fwd, mine, give = refs[: 2 * count], *refs[2 * count : 2 * count + 5]
    wide, pq, o_buf, out_sem = refs[2 * count + 5 :]
    core = info[0]
    zeros = jnp.zeros((SLAB, N), BF16)
    pq[0:SLAB, N:] = zeros
    pq[HALF * SLAB : KEPT * SLAB, N:] = zeros
    pq[KEPT * SLAB :, 0:N] = zeros
    pq[KEPT * SLAB :, N:] = zeros
    stores = []
    for i in range(count):
        t_at = [4 * info[1 + i] + 2 * core, 4 * info[1 + i] + 2 * (1 - core)]
        for j in range(0, SLAB, 2):
            density = jnp.concatenate(
                [
                    pieces[2 * i + m // 8][m % 8] * t_all[t_at[m // 8] + m // 4 % 2, m % 4]
                    for m in (j, j + 1)
                ],
                axis=1,
            )
            out = dot(first[...], density)
            wide[pl.ds(j * FIRST_PITCH, N)] = out[:, :N]
            wide[pl.ds((j + 1) * FIRST_PITCH, N)] = out[:, N:]
        for k in range(KEPT):
            rows = pl.ds(k * SLAB, SLAB)
            pq[rows, 0:N] = wide[pl.ds(k, SLAB, stride=FIRST_PITCH)].astype(BF16)
            if 0 < k < HALF:
                pq[rows, N:] = wide[pl.ds(HALF + k, SLAB, stride=FIRST_PITCH)].astype(BF16)
        for part in range(PLANES // CHUNK):
            out = dot(pq[pl.ds(part * CHUNK * SLAB, CHUNK * SLAB)], lane_fwd[...]).astype(BF16)
            half, ks = part // 3, pl.ds(part % 3 * CHUNK, CHUNK)
            o_buf[i, half, ks, 0] = out[:, :N].reshape(CHUNK, SLAB, N)
            o_buf[i, half, ks, 1] = out[:, N:].reshape(CHUNK, SLAB, N)
        stores.append(pltpu.make_async_copy(o_buf.at[i, core], mine.at[i], out_sem.at[i, 0]))
        stores.append(pltpu.make_async_copy(o_buf.at[i, 1 - core], give.at[i], out_sem.at[i, 1]))
        stores[-1].start()
        stores[-2].start()
    for copy in stores:
        copy.wait()


HBM = pl.BlockSpec(memory_space=pltpu.HBM)
VMEM = pl.BlockSpec(memory_space=pltpu.VMEM)
SMEM = pl.BlockSpec(memory_space=pltpu.SMEM)


def forward(info, pieces, t_all, consts):
    count = len(pieces) // 2
    out = jax.ShapeDtypeStruct((count, SHARE, 2, SLAB, N), BF16)
    return pl.pallas_call(
        functools.partial(forward_kernel, count),
        out_shape=(out, out),
        in_specs=[SMEM] + [VMEM] * (2 * count + 3),
        out_specs=(HBM, HBM),
        scratch_shapes=[
            pltpu.VMEM((SLAB * FIRST_PITCH, N), F32),
            pltpu.VMEM((PLANES * SLAB, 2 * N), BF16),
            pltpu.VMEM((count, 2, SHARE, 2, SLAB, N), BF16),
            pltpu.SemaphoreType.DMA((count, 2)),
        ],
        compiler_params=pltpu.CompilerParams(vmem_limit_bytes=8 * MIB),
        cost_estimate=pl.CostEstimate(
            flops=count * 3500 * 256 * 256, bytes_accessed=count << 21, transcendentals=0
        ),
        name="forward",
    )(info, *pieces, t_all, consts[0], consts[2])


STEPS = ((0, 1, 7), (2, 6), (3, 5, 4))


def middle_kernel(info, *refs):
    own, come = refs[:3], refs[3:6]
    k_hbm, row_fwd, row_inv, mine, give, spec, done, k_buf, in_sem, k_sem, out_sem = refs[6:]
    core, place = info[0], info[1]
    parts = SHARE // CHUNK

    def loads(part):
        ks = pl.ds(part * CHUNK, CHUNK)
        copies = [pltpu.make_async_copy(k_hbm.at[core, ks], k_buf.at[ks], k_sem.at[part])]
        for step, distances in enumerate(STEPS):
            for i, distance in enumerate(distances):
                at = lax.rem(place + 8 - distance, 8)
                for side, (refs_of, row) in enumerate(((own, core), (come, 1 - core))):
                    rows = pl.ds(pl.multiple_of(row * HALF + at % 4 * SLAB, SLAB), SLAB)
                    copies.append(
                        pltpu.make_async_copy(
                            refs_of[step].at[i, ks],
                            spec.at[at // 4, ks, :, rows],
                            in_sem.at[part, distance, side],
                        )
                    )
        return copies

    def stores(part):
        ks = pl.ds(part * CHUNK, CHUNK)
        copies = []
        for side, (ref, row) in enumerate(((mine, core), (give, 1 - core))):
            rows = pl.ds(pl.multiple_of(row * HALF, HALF), HALF)
            copies.append(
                pltpu.make_async_copy(
                    done.at[:, ks, :, rows], ref.at[:, ks], out_sem.at[part, side]
                )
            )
        return copies

    for part in range(parts):
        for copy in loads(part):
            copy.start()
    for part in range(parts):
        for copy in loads(part):
            copy.wait()
        for k in range(part * CHUNK, (part + 1) * CHUNK):
            both = jnp.concatenate(
                [spec[0, k].reshape(2 * N, N), spec[1, k].reshape(2 * N, N)], axis=1
            )
            out = dot(row_fwd[...], both)
            scale = jnp.concatenate([k_buf[k], k_buf[k]], axis=1).astype(F32)
            out = jnp.concatenate([out[:N] * scale, out[N:] * scale], axis=0).astype(BF16)
            out = dot(row_inv[...], out).astype(BF16)
            done[0, k] = out[:, :N].reshape(2, N, N)
            done[1, k] = out[:, N:].reshape(2, N, N)
        for copy in stores(part):
            copy.start()
    for part in range(parts):
        for copy in stores(part):
            copy.wait()


def middle(info, own, come, consts):
    out = jax.ShapeDtypeStruct((2, SHARE, 2, HALF, N), BF16)
    return pl.pallas_call(
        middle_kernel,
        out_shape=(out, out),
        in_specs=[SMEM] + [HBM] * 7 + [VMEM] * 2,
        out_specs=(HBM, HBM),
        scratch_shapes=[
            pltpu.VMEM((2, SHARE, 2, N, N), BF16),
            pltpu.VMEM((2, SHARE, 2, N, N), BF16),
            pltpu.VMEM((SHARE, N, N), BF16),
            pltpu.SemaphoreType.DMA((3, 8, 2)),
            pltpu.SemaphoreType.DMA((3,)),
            pltpu.SemaphoreType.DMA((3, 2)),
        ],
        compiler_params=pltpu.CompilerParams(vmem_limit_bytes=14 * MIB),
        cost_estimate=pl.CostEstimate(
            flops=2 * 17000 * 256 * 256, bytes_accessed=11 << 20, transcendentals=0
        ),
        name="middle",
    )(info, *own, *come, jnp.asarray(coulomb_kernel()), consts[4], consts[5])


def inverse_kernel(info, *refs):
    pieces, own, come, last, lane_inv, field = refs[:16], *refs[16:21]
    s_buf, spec, wide, f_buf, s_sem, in_sem, out_sem = refs[21:]
    core, place = info[0], info[1]
    loads = []
    for part in range(4):
        rows = pl.ds(part * SLAB, SLAB)
        loads.append(
            [
                pltpu.make_async_copy(
                    ref.at[:, :, :, rows], spec.at[part, :, half], in_sem.at[part, side]
                )
                for side, (ref, half) in enumerate(((own, core), (come, 1 - core)))
            ]
        )
    sources = []
    for distance in range(8):
        at = lax.rem(place + 8 - distance, 8)
        for i in range(2):
            sources.append(
                pltpu.make_async_copy(
                    pieces[2 * distance + i], s_buf.at[at // 4, at % 4, i], s_sem.at[distance, i]
                )
            )
    for copy in loads[0] + sources:
        copy.start()
    for copies in loads[1:]:
        for copy in copies:
            copy.start()

    def stores(part):
        return [
            pltpu.make_async_copy(
                f_buf.at[part, p], field.at[pl.ds(4 * part + 2 * bit, 2)], out_sem.at[part, p]
            )
            for p, bit in enumerate((core, 1 - core))
        ]

    for part in range(4):
        for copy in loads[part]:
            copy.wait()
        if part == 0:
            for copy in sources:
                copy.wait()

        for h in range(2):
            for chunk in range(PLANES // CHUNK):
                half, ks = chunk // 3, pl.ds(chunk % 3 * CHUNK, CHUNK)
                p = spec[part, h, half, ks, 0].reshape(CHUNK * SLAB, N)
                q = spec[part, h, half, ks, 1].reshape(CHUNK * SLAB, N)
                out = dot(jnp.concatenate([p, q], axis=1), lane_inv[...])
                base = chunk * CHUNK
                top = min(base + CHUNK, KEPT)
                wide3 = wide.reshape(N, LAST_PITCH, N)
                wide3[pl.ds(base, top - base), 0:SLAB] = out[: (top - base) * SLAB, :N].reshape(top - base, SLAB, N)
                lo, hi = max(base, 1), min(base + CHUNK, HALF)
                wide3[pl.ds(HALF + lo, hi - lo), 0:SLAB] = out[
                    (lo - base) * SLAB : (hi - base) * SLAB, N:
                ].reshape(hi - lo, SLAB, N)
            for j in range(0, SLAB, 2):
                half_spec = jnp.concatenate(
                    [wide[pl.ds(m, N, stride=LAST_PITCH)].astype(BF16) for m in (j, j + 1)], axis=1
                )
                out = dot(last[...], half_spec)
                for m in (j, j + 1):
                    term = out[:, (m - j) * N : (m - j + 1) * N] * s_buf[
                        h, part, m // 8, m % 8
                    ].astype(F32)
                    at = (part, m // 8, m // 4 % 2, m % 4)
                    if h == 1:
                        term = f_buf[at].astype(F32) + term
                    f_buf[at] = term.astype(BF16)
        for copy in stores(part):
            copy.start()
    for part in range(4):
        for copy in stores(part):
            copy.wait()


def inverse(info, pieces, own, come, consts):
    return pl.pallas_call(
        inverse_kernel,
        out_shape=jax.ShapeDtypeStruct((16, 4, N, N), BF16),
        in_specs=[SMEM] + [HBM] * 18 + [VMEM] * 2,
        out_specs=HBM,
        scratch_shapes=[
            pltpu.VMEM((2, 4, 2, SLAB // 2, N, N), BF16),
            pltpu.VMEM((4, 2, 2, SHARE, 2, SLAB, N), BF16),
            pltpu.VMEM((LAST_PITCH * N, N), F32),
            pltpu.VMEM((4, 2, 2, 4, N, N), BF16),
            pltpu.SemaphoreType.DMA((8, 2)),
            pltpu.SemaphoreType.DMA((4, 2)),
            pltpu.SemaphoreType.DMA((4, 2)),
        ],
        compiler_params=pltpu.CompilerParams(vmem_limit_bytes=16 * MIB),
        cost_estimate=pl.CostEstimate(
            flops=2 * 14000 * 256 * 256, bytes_accessed=11 << 20, transcendentals=0
        ),
        name="inverse",
    )(info, *pieces, own, come, consts[1], consts[3])


def along_z(value, by):
    return lax.ppermute(value, ("h", "l"), [(i, (i + by) % 8) for i in range(8)])


def swap_core(value):
    return lax.ppermute(value, "c", [(0, 1), (1, 0)])


TRIPS = [
    ((4 * h + l) * 2 + bit, (l + (2, 6)[bit]) % 8 * 2 + h)
    for h in range(2)
    for l in range(4)
    for bit in range(2)
]


def to_work(value):
    return lax.ppermute(value, ("h", "l", "c"), TRIPS)


def to_owner(value):
    return lax.ppermute(value, ("h", "l", "c"), [(b, a) for a, b in TRIPS])


def over_plane(value):
    return lax.all_to_all(value, ("y", "x"), 0, 0, tiled=True)


def on_device(source_bands, target_bands):
    core = lax.axis_index("c").astype(jnp.int32)
    place = (lax.axis_index("h") * 4 + lax.axis_index("l")).astype(jnp.int32)
    consts = [jnp.asarray(t) for t in tables()]

    planes = source_bands[0].reshape(2, 2, 4, N, N)
    stay = lax.dynamic_index_in_dim(planes, core, 1, keepdims=False).reshape(8, N, N)
    other = lax.dynamic_index_in_dim(planes, 1 - core, 1, keepdims=False).reshape(8, N, N)
    other = swap_core(other)

    target, other = lax.optimization_barrier((target_bands[0], other))
    target = to_work(target)

    at = {0: (stay, other)}
    first = along_z(stay, 1), along_z(stay, -1)
    target = lax.optimization_barrier((target, *first))[0]
    t_all = over_plane(jnp.broadcast_to(target[None], (16, 4, N, N)))

    at[1] = (first[0], along_z(other, 1))
    at[7] = (first[1], along_z(other, -1))
    for k in range(2, 4):
        up, down = at[k - 1], at[9 - k]
        at[k] = tuple(along_z(piece, 1) for piece in up)
        at[8 - k] = tuple(along_z(piece, -1) for piece in down)

    own, come = [], []
    for distances in STEPS:
        if 4 in distances:
            up, down, own[0] = lax.optimization_barrier((at[3][0], at[5][1], own[0]))
            last = (along_z(up, 1), along_z(down, -1))
            *at[4], own[1] = lax.optimization_barrier((*last, own[1]))
        info = jnp.stack([core] + [(place + 8 - d) % 4 for d in distances])
        mine, give = forward(info, [p for d in distances for p in at[d]], t_all, consts)
        own.append(mine)
        come.append(swap_core(give))

    info = jnp.stack([core, place])
    mine, give = middle(info, own, come, consts)
    field = inverse(info, [p for d in range(8) for p in at[d]], mine, swap_core(give), consts)
    field = jnp.sum(over_plane(field).astype(F32), axis=0).astype(BF16)
    return to_owner(field).astype(F32)[None]


def solution(mesh):
    fine = Mesh(mesh.devices.reshape(4, 4, 2, 4, 2), ("y", "x", "h", "l", "c"))
    src, tgt = ("y", "x", "h"), ("l", "c")
    return jax.shard_map(
        on_device,
        mesh=fine,
        in_specs=(P(src, tgt, None, None), P(tgt, src, None, None)),
        out_specs=P(tgt, src, None, None),
        check_vma=False,
    )
```

```python
import functools
import math

import jax
import jax.numpy as jnp
import ml_dtypes
import numpy as np
from jax import lax
from jax.experimental import pallas as pl
from jax.experimental.pallas import tpu as pltpu
from jax.sharding import Mesh
from jax.sharding import PartitionSpec as P

N = 128
HALF = N // 2
KEPT = HALF + 1
SLAB = 16
PLANES = KEPT + 1
SHARE = PLANES // 2
CHUNK = 11
FIRST_PITCH = N + 8
LAST_PITCH = SLAB + 8
FRACTION = 0.25
CELL = 59.2
MIB = 1024 * 1024
BF16 = jnp.bfloat16
F32 = jnp.float32


def tables():
    counter = np.arange(N)
    angles = (2.0 * math.pi / N) * (counter[:, None] * counter[None, :] % N)
    cos = np.cos(angles)
    sin = np.sin(angles)
    first = np.concatenate([cos[:KEPT], -sin[1:HALF]], axis=0)
    weight = np.full(N, 2.0)
    weight[0] = weight[HALF] = 1.0
    last = -FRACTION * np.concatenate(
        [cos[:, :KEPT] * weight[None, :KEPT], -2.0 * sin[:, 1:HALF]], axis=1
    )
    forward = np.block([[cos, -sin], [sin, cos]])
    inverse = np.block([[cos, sin], [-sin, cos]])
    x = np.arange(N).reshape(4, 2, 2, 2, 4)
    order = np.concatenate([x[:, :, :, c][:, [c, 1 - c]].reshape(HALF) for c in range(2)])
    both = np.concatenate([order, order + N])
    every = (first, last, forward, inverse, forward.T[:, both], inverse.T[both, :])
    return [np.asarray(t, np.float32).astype(ml_dtypes.bfloat16) for t in every]


def coulomb_kernel():
    counter = np.arange(N)
    wrapped = np.where(counter < HALF, counter, counter - N)
    wave = (2.0 * math.pi / CELL * wrapped) ** 2
    wave_sq = wave[:KEPT, None, None] + wave[None, :, None] + wave[None, None, :]
    radius = CELL * (3.0 / (4.0 * math.pi)) ** (1.0 / 3.0)
    safe_sq = np.where(wave_sq > 0, wave_sq, 1.0)
    values = np.where(
        wave_sq > 0,
        4.0 * math.pi * (1.0 - np.cos(np.sqrt(safe_sq) * radius)) / safe_sq,
        2.0 * math.pi * radius * radius,
    )
    values = values / N**3
    values = np.concatenate([values, np.zeros((1, N, N))]).astype(np.float32)
    return values.astype(ml_dtypes.bfloat16).reshape(2, SHARE, N, N)


def dot(left, right):
    return jnp.dot(left, right, preferred_element_type=F32)


def forward_kernel(count, info, *refs):
    pieces, t_all, first, lane_fwd, mine, give = refs[: 2 * count], *refs[2 * count : 2 * count + 5]
    wide, pq, o_buf, out_sem = refs[2 * count + 5 :]
    core = info[0]
    zeros = jnp.zeros((SLAB, N), BF16)
    pq[0:SLAB, N:] = zeros
    pq[HALF * SLAB : KEPT * SLAB, N:] = zeros
    pq[KEPT * SLAB :, 0:N] = zeros
    pq[KEPT * SLAB :, N:] = zeros
    stores = []
    for i in range(count):
        t_at = [4 * info[1 + i] + 2 * core, 4 * info[1 + i] + 2 * (1 - core)]
        for j in range(0, SLAB, 2):
            density = jnp.concatenate(
                [
                    pieces[2 * i + m // 8][m % 8] * t_all[t_at[m // 8] + m // 4 % 2, m % 4]
                    for m in (j, j + 1)
                ],
                axis=1,
            )
            out = dot(first[...], density)
            wide[pl.ds(j * FIRST_PITCH, N)] = out[:, :N]
            wide[pl.ds((j + 1) * FIRST_PITCH, N)] = out[:, N:]
        for k in range(KEPT):
            rows = pl.ds(k * SLAB, SLAB)
            pq[rows, 0:N] = wide[pl.ds(k, SLAB, stride=FIRST_PITCH)].astype(BF16)
            if 0 < k < HALF:
                pq[rows, N:] = wide[pl.ds(HALF + k, SLAB, stride=FIRST_PITCH)].astype(BF16)
        for part in range(PLANES // CHUNK):
            out = dot(pq[pl.ds(part * CHUNK * SLAB, CHUNK * SLAB)], lane_fwd[...]).astype(BF16)
            half, ks = part // 3, pl.ds(part % 3 * CHUNK, CHUNK)
            o_buf[i, half, ks, 0] = out[:, :N].reshape(CHUNK, SLAB, N)
            o_buf[i, half, ks, 1] = out[:, N:].reshape(CHUNK, SLAB, N)
        stores.append(pltpu.make_async_copy(o_buf.at[i, core], mine.at[i], out_sem.at[i, 0]))
        stores.append(pltpu.make_async_copy(o_buf.at[i, 1 - core], give.at[i], out_sem.at[i, 1]))
        stores[-1].start()
        stores[-2].start()
    for copy in stores:
        copy.wait()


HBM = pl.BlockSpec(memory_space=pltpu.HBM)
VMEM = pl.BlockSpec(memory_space=pltpu.VMEM)
SMEM = pl.BlockSpec(memory_space=pltpu.SMEM)


def forward(info, pieces, t_all, consts):
    count = len(pieces) // 2
    out = jax.ShapeDtypeStruct((count, SHARE, 2, SLAB, N), BF16)
    return pl.pallas_call(
        functools.partial(forward_kernel, count),
        out_shape=(out, out),
        in_specs=[SMEM] + [VMEM] * (2 * count + 3),
        out_specs=(HBM, HBM),
        scratch_shapes=[
            pltpu.VMEM((SLAB * FIRST_PITCH, N), F32),
            pltpu.VMEM((PLANES * SLAB, 2 * N), BF16),
            pltpu.VMEM((count, 2, SHARE, 2, SLAB, N), BF16),
            pltpu.SemaphoreType.DMA((count, 2)),
        ],
        compiler_params=pltpu.CompilerParams(vmem_limit_bytes=8 * MIB),
        cost_estimate=pl.CostEstimate(
            flops=count * 3500 * 256 * 256, bytes_accessed=count << 21, transcendentals=0
        ),
        name="forward",
    )(info, *pieces, t_all, consts[0], consts[2])


STEPS = ((0, 1, 7), (2, 6), (3, 5, 4))


def middle_kernel(info, *refs):
    own, come = refs[:3], refs[3:6]
    k_hbm, row_fwd, row_inv, mine, give, spec, done, k_buf, in_sem, k_sem, out_sem = refs[6:]
    core, place = info[0], info[1]
    parts = SHARE // CHUNK

    def loads(part):
        ks = pl.ds(part * CHUNK, CHUNK)
        copies = [pltpu.make_async_copy(k_hbm.at[core, ks], k_buf.at[ks], k_sem.at[part])]
        for step, distances in enumerate(STEPS):
            for i, distance in enumerate(distances):
                at = lax.rem(place + 8 - distance, 8)
                for side, (refs_of, row) in enumerate(((own, core), (come, 1 - core))):
                    rows = pl.ds(pl.multiple_of(row * HALF + at % 4 * SLAB, SLAB), SLAB)
                    copies.append(
                        pltpu.make_async_copy(
                            refs_of[step].at[i, ks],
                            spec.at[at // 4, ks, :, rows],
                            in_sem.at[part, distance, side],
                        )
                    )
        return copies

    def stores(part):
        ks = pl.ds(part * CHUNK, CHUNK)
        copies = []
        for side, (ref, row) in enumerate(((mine, core), (give, 1 - core))):
            rows = pl.ds(pl.multiple_of(row * HALF, HALF), HALF)
            copies.append(
                pltpu.make_async_copy(
                    done.at[:, ks, :, rows], ref.at[:, ks], out_sem.at[part, side]
                )
            )
        return copies

    for part in range(parts):
        for copy in loads(part):
            copy.start()
    for part in range(parts):
        for copy in loads(part):
            copy.wait()
        for k in range(part * CHUNK, (part + 1) * CHUNK):
            both = jnp.concatenate(
                [spec[0, k].reshape(2 * N, N), spec[1, k].reshape(2 * N, N)], axis=1
            )
            out = dot(row_fwd[...], both)
            scale = jnp.concatenate([k_buf[k], k_buf[k]], axis=1).astype(F32)
            out = jnp.concatenate([out[:N] * scale, out[N:] * scale], axis=0).astype(BF16)
            out = dot(row_inv[...], out).astype(BF16)
            done[0, k] = out[:, :N].reshape(2, N, N)
            done[1, k] = out[:, N:].reshape(2, N, N)
        for copy in stores(part):
            copy.start()
    for part in range(parts):
        for copy in stores(part):
            copy.wait()


def middle(info, own, come, consts):
    out = jax.ShapeDtypeStruct((2, SHARE, 2, HALF, N), BF16)
    return pl.pallas_call(
        middle_kernel,
        out_shape=(out, out),
        in_specs=[SMEM] + [HBM] * 7 + [VMEM] * 2,
        out_specs=(HBM, HBM),
        scratch_shapes=[
            pltpu.VMEM((2, SHARE, 2, N, N), BF16),
            pltpu.VMEM((2, SHARE, 2, N, N), BF16),
            pltpu.VMEM((SHARE, N, N), BF16),
            pltpu.SemaphoreType.DMA((3, 8, 2)),
            pltpu.SemaphoreType.DMA((3,)),
            pltpu.SemaphoreType.DMA((3, 2)),
        ],
        compiler_params=pltpu.CompilerParams(vmem_limit_bytes=14 * MIB),
        cost_estimate=pl.CostEstimate(
            flops=2 * 17000 * 256 * 256, bytes_accessed=11 << 20, transcendentals=0
        ),
        name="middle",
    )(info, *own, *come, jnp.asarray(coulomb_kernel()), consts[4], consts[5])


def inverse_kernel(info, *refs):
    pieces, own, come, last, lane_inv, field = refs[:16], *refs[16:21]
    s_buf, spec, wide, f_buf, s_sem, in_sem, out_sem = refs[21:]
    core, place = info[0], info[1]
    loads = []
    for part in range(4):
        rows = pl.ds(part * SLAB, SLAB)
        loads.append(
            [
                pltpu.make_async_copy(
                    ref.at[:, :, :, rows], spec.at[part, :, half], in_sem.at[part, side]
                )
                for side, (ref, half) in enumerate(((own, core), (come, 1 - core)))
            ]
        )
    sources = []
    for distance in range(8):
        at = lax.rem(place + 8 - distance, 8)
        for i in range(2):
            sources.append(
                pltpu.make_async_copy(
                    pieces[2 * distance + i], s_buf.at[at // 4, at % 4, i], s_sem.at[distance, i]
                )
            )
    for copy in loads[0] + sources:
        copy.start()
    for copies in loads[1:]:
        for copy in copies:
            copy.start()

    def stores(part):
        return [
            pltpu.make_async_copy(
                f_buf.at[part, p], field.at[pl.ds(4 * part + 2 * bit, 2)], out_sem.at[part, p]
            )
            for p, bit in enumerate((core, 1 - core))
        ]

    for part in range(4):
        for copy in loads[part]:
            copy.wait()
        for h in range(2):
            distance = lax.rem(place + 8 - (4 * h + part), 8)
            for i in range(2):
                pltpu.make_async_copy(
                    pieces[i], s_buf.at[h, part, i], s_sem.at[distance, i]
                ).wait()

        for h in range(2):
            for chunk in range(PLANES // CHUNK):
                half, ks = chunk // 3, pl.ds(chunk % 3 * CHUNK, CHUNK)
                p = spec[part, h, half, ks, 0].reshape(CHUNK * SLAB, N)
                q = spec[part, h, half, ks, 1].reshape(CHUNK * SLAB, N)
                out = dot(jnp.concatenate([p, q], axis=1), lane_inv[...])
                base = chunk * CHUNK
                top = min(base + CHUNK, KEPT)
                wide3 = wide.reshape(N, LAST_PITCH, N)
                wide3[pl.ds(base, top - base), 0:SLAB] = out[: (top - base) * SLAB, :N].reshape(top - base, SLAB, N)
                lo, hi = max(base, 1), min(base + CHUNK, HALF)
                wide3[pl.ds(HALF + lo, hi - lo), 0:SLAB] = out[
                    (lo - base) * SLAB : (hi - base) * SLAB, N:
                ].reshape(hi - lo, SLAB, N)
            for j in range(0, SLAB, 2):
                half_spec = jnp.concatenate(
                    [wide[pl.ds(m, N, stride=LAST_PITCH)].astype(BF16) for m in (j, j + 1)], axis=1
                )
                out = dot(last[...], half_spec)
                for m in (j, j + 1):
                    term = out[:, (m - j) * N : (m - j + 1) * N] * s_buf[
                        h, part, m // 8, m % 8
                    ].astype(F32)
                    at = (part, m // 8, m // 4 % 2, m % 4)
                    if h == 1:
                        term = f_buf[at].astype(F32) + term
                    f_buf[at] = term.astype(BF16)
        for copy in stores(part):
            copy.start()
    for part in range(4):
        for copy in stores(part):
            copy.wait()


def inverse(info, pieces, own, come, consts):
    return pl.pallas_call(
        inverse_kernel,
        out_shape=jax.ShapeDtypeStruct((16, 4, N, N), BF16),
        in_specs=[SMEM] + [HBM] * 18 + [VMEM] * 2,
        out_specs=HBM,
        scratch_shapes=[
            pltpu.VMEM((2, 4, 2, SLAB // 2, N, N), BF16),
            pltpu.VMEM((4, 2, 2, SHARE, 2, SLAB, N), BF16),
            pltpu.VMEM((LAST_PITCH * N, N), F32),
            pltpu.VMEM((4, 2, 2, 4, N, N), BF16),
            pltpu.SemaphoreType.DMA((8, 2)),
            pltpu.SemaphoreType.DMA((4, 2)),
            pltpu.SemaphoreType.DMA((4, 2)),
        ],
        compiler_params=pltpu.CompilerParams(vmem_limit_bytes=16 * MIB),
        cost_estimate=pl.CostEstimate(
            flops=2 * 14000 * 256 * 256, bytes_accessed=11 << 20, transcendentals=0
        ),
        name="inverse",
    )(info, *pieces, own, come, consts[1], consts[3])


def along_z(value, by):
    return lax.ppermute(value, ("h", "l"), [(i, (i + by) % 8) for i in range(8)])


def swap_core(value):
    return lax.ppermute(value, "c", [(0, 1), (1, 0)])


TRIPS = [
    ((4 * h + l) * 2 + bit, (l + (2, 6)[bit]) % 8 * 2 + h)
    for h in range(2)
    for l in range(4)
    for bit in range(2)
]


def to_work(value):
    return lax.ppermute(value, ("h", "l", "c"), TRIPS)


def to_owner(value):
    return lax.ppermute(value, ("h", "l", "c"), [(b, a) for a, b in TRIPS])


def over_plane(value):
    return lax.all_to_all(value, ("y", "x"), 0, 0, tiled=True)


def on_device(source_bands, target_bands):
    core = lax.axis_index("c").astype(jnp.int32)
    place = (lax.axis_index("h") * 4 + lax.axis_index("l")).astype(jnp.int32)
    consts = [jnp.asarray(t) for t in tables()]

    planes = source_bands[0].reshape(2, 2, 4, N, N)
    stay = lax.dynamic_index_in_dim(planes, core, 1, keepdims=False).reshape(8, N, N)
    other = lax.dynamic_index_in_dim(planes, 1 - core, 1, keepdims=False).reshape(8, N, N)
    other = swap_core(other)

    target, other = lax.optimization_barrier((target_bands[0], other))
    target = to_work(target)

    at = {0: (stay, other)}
    first = along_z(stay, 1), along_z(stay, -1)
    t_all = over_plane(jnp.broadcast_to(target[None], (16, 4, N, N)))

    at[1] = (first[0], along_z(other, 1))
    at[7] = (first[1], along_z(other, -1))
    for k in range(2, 4):
        up, down = at[k - 1], at[9 - k]
        at[k] = tuple(along_z(piece, 1) for piece in up)
        at[8 - k] = tuple(along_z(piece, -1) for piece in down)

    own, come = [], []
    for distances in STEPS:
        if 4 in distances:
            up, down, own[0] = lax.optimization_barrier((at[3][0], at[5][1], own[0]))
            last = (along_z(up, 1), along_z(down, -1))
            *at[4], own[1] = lax.optimization_barrier((*last, own[1]))
        info = jnp.stack([core] + [(place + 8 - d) % 4 for d in distances])
        mine, give = forward(info, [p for d in distances for p in at[d]], t_all, consts)
        own.append(mine)
        come.append(swap_core(give))

    info = jnp.stack([core, place])
    mine, give = middle(info, own, come, consts)
    field = inverse(info, [p for d in range(8) for p in at[d]], mine, swap_core(give), consts)
    field = jnp.sum(over_plane(field).astype(F32), axis=0).astype(BF16)
    return to_owner(field).astype(F32)[None]


def solution(mesh):
    fine = Mesh(mesh.devices.reshape(4, 4, 2, 4, 2), ("y", "x", "h", "l", "c"))
    src, tgt = ("y", "x", "h"), ("l", "c")
    return jax.shard_map(
        on_device,
        mesh=fine,
        in_specs=(P(src, tgt, None, None), P(tgt, src, None, None)),
        out_specs=P(tgt, src, None, None),
        check_vma=False,
    )
```

```python
import functools
import math

import jax
import jax.numpy as jnp
import ml_dtypes
import numpy as np
from jax import lax
from jax.experimental import pallas as pl
from jax.experimental.pallas import tpu as pltpu
from jax.sharding import Mesh
from jax.sharding import PartitionSpec as P

N = 128
HALF = N // 2
KEPT = HALF + 1
SLAB = 16
PLANES = KEPT + 1
SHARE = PLANES // 2
CHUNK = 11
FIRST_PITCH = N + 8
LAST_PITCH = SLAB + 8
FRACTION = 0.25
CELL = 59.2
MIB = 1024 * 1024
BF16 = jnp.bfloat16
F32 = jnp.float32


def tables():
    counter = np.arange(N)
    angles = (2.0 * math.pi / N) * (counter[:, None] * counter[None, :] % N)
    cos = np.cos(angles)
    sin = np.sin(angles)
    first = np.concatenate([cos[:KEPT], -sin[1:HALF]], axis=0)
    weight = np.full(N, 2.0)
    weight[0] = weight[HALF] = 1.0
    last = -FRACTION * np.concatenate(
        [cos[:, :KEPT] * weight[None, :KEPT], -2.0 * sin[:, 1:HALF]], axis=1
    )
    forward = np.block([[cos, -sin], [sin, cos]])
    inverse = np.block([[cos, sin], [-sin, cos]])
    x = np.arange(N).reshape(4, 2, 2, 2, 4)
    order = np.concatenate([x[:, :, :, c][:, [c, 1 - c]].reshape(HALF) for c in range(2)])
    both = np.concatenate([order, order + N])
    every = (first, last, forward, inverse, forward.T[:, both], inverse.T[both, :])
    return [np.asarray(t, np.float32).astype(ml_dtypes.bfloat16) for t in every]


def coulomb_kernel():
    counter = np.arange(N)
    wrapped = np.where(counter < HALF, counter, counter - N)
    wave = (2.0 * math.pi / CELL * wrapped) ** 2
    wave_sq = wave[:KEPT, None, None] + wave[None, :, None] + wave[None, None, :]
    radius = CELL * (3.0 / (4.0 * math.pi)) ** (1.0 / 3.0)
    safe_sq = np.where(wave_sq > 0, wave_sq, 1.0)
    values = np.where(
        wave_sq > 0,
        4.0 * math.pi * (1.0 - np.cos(np.sqrt(safe_sq) * radius)) / safe_sq,
        2.0 * math.pi * radius * radius,
    )
    values = values / N**3
    values = np.concatenate([values, np.zeros((1, N, N))]).astype(np.float32)
    return values.astype(ml_dtypes.bfloat16).reshape(2, SHARE, N, N)


def dot(left, right):
    return jnp.dot(left, right, preferred_element_type=F32)


def forward_kernel(count, info, *refs):
    pieces, t_all, first, lane_fwd, mine, give = refs[: 2 * count], *refs[2 * count : 2 * count + 5]
    wide, pq, o_buf, out_sem = refs[2 * count + 5 :]
    core = info[0]
    zeros = jnp.zeros((SLAB, N), BF16)
    pq[0:SLAB, N:] = zeros
    pq[HALF * SLAB : KEPT * SLAB, N:] = zeros
    pq[KEPT * SLAB :, 0:N] = zeros
    pq[KEPT * SLAB :, N:] = zeros
    stores = []
    for i in range(count):
        t_at = [4 * info[1 + i] + 2 * core, 4 * info[1 + i] + 2 * (1 - core)]
        for j in range(0, SLAB, 2):
            density = jnp.concatenate(
                [
                    pieces[2 * i + m // 8][m % 8] * t_all[t_at[m // 8] + m // 4 % 2, m % 4]
                    for m in (j, j + 1)
                ],
                axis=1,
            )
            out = dot(first[...], density)
            wide[pl.ds(j * FIRST_PITCH, N)] = out[:, :N]
            wide[pl.ds((j + 1) * FIRST_PITCH, N)] = out[:, N:]
        for k in range(KEPT):
            rows = pl.ds(k * SLAB, SLAB)
            pq[rows, 0:N] = wide[pl.ds(k, SLAB, stride=FIRST_PITCH)].astype(BF16)
            if 0 < k < HALF:
                pq[rows, N:] = wide[pl.ds(HALF + k, SLAB, stride=FIRST_PITCH)].astype(BF16)
        for part in range(PLANES // CHUNK):
            out = dot(pq[pl.ds(part * CHUNK * SLAB, CHUNK * SLAB)], lane_fwd[...]).astype(BF16)
            half, ks = part // 3, pl.ds(part % 3 * CHUNK, CHUNK)
            o_buf[i, half, ks, 0] = out[:, :N].reshape(CHUNK, SLAB, N)
            o_buf[i, half, ks, 1] = out[:, N:].reshape(CHUNK, SLAB, N)
        stores.append(pltpu.make_async_copy(o_buf.at[i, core], mine.at[i], out_sem.at[i, 0]))
        stores.append(pltpu.make_async_copy(o_buf.at[i, 1 - core], give.at[i], out_sem.at[i, 1]))
        stores[-1].start()
        stores[-2].start()
    for copy in stores:
        copy.wait()


HBM = pl.BlockSpec(memory_space=pltpu.HBM)
VMEM = pl.BlockSpec(memory_space=pltpu.VMEM)
SMEM = pl.BlockSpec(memory_space=pltpu.SMEM)


def forward(info, pieces, t_all, consts):
    count = len(pieces) // 2
    out = jax.ShapeDtypeStruct((count, SHARE, 2, SLAB, N), BF16)
    return pl.pallas_call(
        functools.partial(forward_kernel, count),
        out_shape=(out, out),
        in_specs=[SMEM] + [VMEM] * (2 * count + 3),
        out_specs=(HBM, HBM),
        scratch_shapes=[
            pltpu.VMEM((SLAB * FIRST_PITCH, N), F32),
            pltpu.VMEM((PLANES * SLAB, 2 * N), BF16),
            pltpu.VMEM((count, 2, SHARE, 2, SLAB, N), BF16),
            pltpu.SemaphoreType.DMA((count, 2)),
        ],
        compiler_params=pltpu.CompilerParams(vmem_limit_bytes=8 * MIB),
        cost_estimate=pl.CostEstimate(
            flops=count * 3500 * 256 * 256, bytes_accessed=count << 21, transcendentals=0
        ),
        name="forward",
    )(info, *pieces, t_all, consts[0], consts[2])


STEPS = ((0, 1, 7), (2, 6), (3, 5, 4))


def middle_kernel(info, *refs):
    own, come = refs[:3], refs[3:6]
    k_hbm, row_fwd, row_inv, mine, give, spec, done, k_buf, in_sem, k_sem, out_sem = refs[6:]
    core, place = info[0], info[1]
    parts = SHARE // CHUNK

    def loads(part):
        ks = pl.ds(part * CHUNK, CHUNK)
        copies = [pltpu.make_async_copy(k_hbm.at[core, ks], k_buf.at[ks], k_sem.at[part])]
        for step, distances in enumerate(STEPS):
            for i, distance in enumerate(distances):
                at = lax.rem(place + 8 - distance, 8)
                for side, (refs_of, row) in enumerate(((own, core), (come, 1 - core))):
                    rows = pl.ds(pl.multiple_of(row * HALF + at % 4 * SLAB, SLAB), SLAB)
                    copies.append(
                        pltpu.make_async_copy(
                            refs_of[step].at[i, ks],
                            spec.at[at // 4, ks, :, rows],
                            in_sem.at[part, distance, side],
                        )
                    )
        return copies

    def stores(part):
        ks = pl.ds(part * CHUNK, CHUNK)
        copies = []
        for side, (ref, row) in enumerate(((mine, core), (give, 1 - core))):
            rows = pl.ds(pl.multiple_of(row * HALF, HALF), HALF)
            copies.append(
                pltpu.make_async_copy(
                    done.at[:, ks, :, rows], ref.at[:, ks], out_sem.at[part, side]
                )
            )
        return copies

    for part in range(parts):
        for copy in loads(part):
            copy.start()
    for part in range(parts):
        for copy in loads(part):
            copy.wait()
        for k in range(part * CHUNK, (part + 1) * CHUNK):
            both = jnp.concatenate(
                [spec[0, k].reshape(2 * N, N), spec[1, k].reshape(2 * N, N)], axis=1
            )
            out = dot(row_fwd[...], both)
            scale = jnp.concatenate([k_buf[k], k_buf[k]], axis=1).astype(F32)
            out = jnp.concatenate([out[:N] * scale, out[N:] * scale], axis=0).astype(BF16)
            out = dot(row_inv[...], out).astype(BF16)
            done[0, k] = out[:, :N].reshape(2, N, N)
            done[1, k] = out[:, N:].reshape(2, N, N)
        for copy in stores(part):
            copy.start()
    for part in range(parts):
        for copy in stores(part):
            copy.wait()


def middle(info, own, come, consts):
    out = jax.ShapeDtypeStruct((2, SHARE, 2, HALF, N), BF16)
    return pl.pallas_call(
        middle_kernel,
        out_shape=(out, out),
        in_specs=[SMEM] + [HBM] * 7 + [VMEM] * 2,
        out_specs=(HBM, HBM),
        scratch_shapes=[
            pltpu.VMEM((2, SHARE, 2, N, N), BF16),
            pltpu.VMEM((2, SHARE, 2, N, N), BF16),
            pltpu.VMEM((SHARE, N, N), BF16),
            pltpu.SemaphoreType.DMA((3, 8, 2)),
            pltpu.SemaphoreType.DMA((3,)),
            pltpu.SemaphoreType.DMA((3, 2)),
        ],
        compiler_params=pltpu.CompilerParams(vmem_limit_bytes=14 * MIB),
        cost_estimate=pl.CostEstimate(
            flops=2 * 17000 * 256 * 256, bytes_accessed=11 << 20, transcendentals=0
        ),
        name="middle",
    )(info, *own, *come, jnp.asarray(coulomb_kernel()), consts[4], consts[5])


def inverse_kernel(info, *refs):
    pieces, own, come, last, lane_inv, field = refs[:16], *refs[16:21]
    s_buf, spec, wide, f_buf, s_sem, in_sem, out_sem = refs[21:]
    core, place = info[0], info[1]
    loads = []
    for part in range(4):
        rows = pl.ds(part * SLAB, SLAB)
        loads.append(
            [
                pltpu.make_async_copy(
                    ref.at[:, :, :, rows], spec.at[part, :, half], in_sem.at[part, side]
                )
                for side, (ref, half) in enumerate(((own, core), (come, 1 - core)))
            ]
        )
    sources = []
    for distance in range(8):
        at = lax.rem(place + 8 - distance, 8)
        for i in range(2):
            sources.append(
                pltpu.make_async_copy(
                    pieces[2 * distance + i], s_buf.at[at // 4, at % 4, i], s_sem.at[distance, i]
                )
            )
    for copy in loads[0] + sources:
        copy.start()
    for copies in loads[1:]:
        for copy in copies:
            copy.start()

    def stores(part):
        return [
            pltpu.make_async_copy(
                f_buf.at[part, p], field.at[pl.ds(4 * part + 2 * bit, 2)], out_sem.at[part, p]
            )
            for p, bit in enumerate((core, 1 - core))
        ]

    for part in range(4):
        for copy in loads[part]:
            copy.wait()
        for h in range(2):
            distance = lax.rem(place + 8 - (4 * h + part), 8)
            for i in range(2):
                pltpu.make_async_copy(
                    pieces[i], s_buf.at[h, part, i], s_sem.at[distance, i]
                ).wait()

        for h in range(2):
            for chunk in range(PLANES // CHUNK):
                half, ks = chunk // 3, pl.ds(chunk % 3 * CHUNK, CHUNK)
                p = spec[part, h, half, ks, 0].reshape(CHUNK * SLAB, N)
                q = spec[part, h, half, ks, 1].reshape(CHUNK * SLAB, N)
                out = dot(jnp.concatenate([p, q], axis=1), lane_inv[...])
                base = chunk * CHUNK
                top = min(base + CHUNK, KEPT)
                wide3 = wide.reshape(N, LAST_PITCH, N)
                wide3[pl.ds(base, top - base), 0:SLAB] = out[: (top - base) * SLAB, :N].reshape(top - base, SLAB, N)
                lo, hi = max(base, 1), min(base + CHUNK, HALF)
                wide3[pl.ds(HALF + lo, hi - lo), 0:SLAB] = out[
                    (lo - base) * SLAB : (hi - base) * SLAB, N:
                ].reshape(hi - lo, SLAB, N)
            for j in range(0, SLAB, 2):
                half_spec = jnp.concatenate(
                    [wide[pl.ds(m, N, stride=LAST_PITCH)].astype(BF16) for m in (j, j + 1)], axis=1
                )
                out = dot(last[...], half_spec)
                for m in (j, j + 1):
                    term = out[:, (m - j) * N : (m - j + 1) * N] * s_buf[
                        h, part, m // 8, m % 8
                    ].astype(F32)
                    at = (part, m // 8, m // 4 % 2, m % 4)
                    if h == 1:
                        term = f_buf[at].astype(F32) + term
                    f_buf[at] = term.astype(BF16)
        for copy in stores(part):
            copy.start()
    for part in range(4):
        for copy in stores(part):
            copy.wait()


def inverse(info, pieces, own, come, consts):
    return pl.pallas_call(
        inverse_kernel,
        out_shape=jax.ShapeDtypeStruct((16, 4, N, N), BF16),
        in_specs=[SMEM] + [HBM] * 18 + [VMEM] * 2,
        out_specs=HBM,
        scratch_shapes=[
            pltpu.VMEM((2, 4, 2, SLAB // 2, N, N), BF16),
            pltpu.VMEM((4, 2, 2, SHARE, 2, SLAB, N), BF16),
            pltpu.VMEM((LAST_PITCH * N, N), F32),
            pltpu.VMEM((4, 2, 2, 4, N, N), BF16),
            pltpu.SemaphoreType.DMA((8, 2)),
            pltpu.SemaphoreType.DMA((4, 2)),
            pltpu.SemaphoreType.DMA((4, 2)),
        ],
        compiler_params=pltpu.CompilerParams(vmem_limit_bytes=16 * MIB),
        cost_estimate=pl.CostEstimate(
            flops=2 * 14000 * 256 * 256, bytes_accessed=11 << 20, transcendentals=0
        ),
        name="inverse",
    )(info, *pieces, own, come, consts[1], consts[3])


def along_z(value, by):
    return lax.ppermute(value, ("h", "l"), [(i, (i + by) % 8) for i in range(8)])


def swap_core(value):
    return lax.ppermute(value, "c", [(0, 1), (1, 0)])


TRIPS = [
    ((4 * h + l) * 2 + bit, (l + (2, 6)[bit]) % 8 * 2 + h)
    for h in range(2)
    for l in range(4)
    for bit in range(2)
]


def to_work(value):
    return lax.ppermute(value, ("h", "l", "c"), TRIPS)


def to_owner(value):
    return lax.ppermute(value, ("h", "l", "c"), [(b, a) for a, b in TRIPS])


def over_plane(value):
    return lax.all_to_all(value, ("y", "x"), 0, 0, tiled=True)


def on_device(source_bands, target_bands):
    core = lax.axis_index("c").astype(jnp.int32)
    place = (lax.axis_index("h") * 4 + lax.axis_index("l")).astype(jnp.int32)
    consts = [jnp.asarray(t) for t in tables()]

    planes = source_bands[0].reshape(2, 2, 4, N, N)
    stay = lax.dynamic_index_in_dim(planes, core, 1, keepdims=False).reshape(8, N, N)
    other = lax.dynamic_index_in_dim(planes, 1 - core, 1, keepdims=False).reshape(8, N, N)
    other = swap_core(other)

    target = to_work(target_bands[0])

    at = {0: (stay, other)}
    first = along_z(stay, 1), along_z(stay, -1)
    t_all = over_plane(jnp.broadcast_to(target[None], (16, 4, N, N)))

    at[1] = (first[0], along_z(other, 1))
    at[7] = (first[1], along_z(other, -1))
    for k in range(2, 4):
        up, down = at[k - 1], at[9 - k]
        at[k] = tuple(along_z(piece, 1) for piece in up)
        at[8 - k] = tuple(along_z(piece, -1) for piece in down)

    own, come = [], []
    for distances in STEPS:
        if 4 in distances:
            up, down, own[0] = lax.optimization_barrier((at[3][0], at[5][1], own[0]))
            last = (along_z(up, 1), along_z(down, -1))
            *at[4], own[1] = lax.optimization_barrier((*last, own[1]))
        info = jnp.stack([core] + [(place + 8 - d) % 4 for d in distances])
        mine, give = forward(info, [p for d in distances for p in at[d]], t_all, consts)
        own.append(mine)
        come.append(swap_core(give))

    info = jnp.stack([core, place])
    mine, give = middle(info, own, come, consts)
    field = inverse(info, [p for d in range(8) for p in at[d]], mine, swap_core(give), consts)
    field = jnp.sum(over_plane(field).astype(F32), axis=0).astype(BF16)
    return to_owner(field).astype(F32)[None]


def solution(mesh):
    fine = Mesh(mesh.devices.reshape(4, 4, 2, 4, 2), ("y", "x", "h", "l", "c"))
    src, tgt = ("y", "x", "h"), ("l", "c")
    return jax.shard_map(
        on_device,
        mesh=fine,
        in_specs=(P(src, tgt, None, None), P(tgt, src, None, None)),
        out_specs=P(tgt, src, None, None),
        check_vma=False,
    )
```

```python
import functools
import math

import jax
import jax.numpy as jnp
import ml_dtypes
import numpy as np
from jax import lax
from jax.experimental import pallas as pl
from jax.experimental.pallas import tpu as pltpu
from jax.sharding import Mesh
from jax.sharding import PartitionSpec as P

N = 128
HALF = N // 2
KEPT = HALF + 1
SLAB = 16
PLANES = KEPT + 1
SHARE = PLANES // 2
CHUNK = 11
FIRST_PITCH = N + 8
LAST_PITCH = SLAB + 8
FRACTION = 0.25
CELL = 59.2
MIB = 1024 * 1024
BF16 = jnp.bfloat16
F32 = jnp.float32


def tables():
    counter = np.arange(N)
    angles = (2.0 * math.pi / N) * (counter[:, None] * counter[None, :] % N)
    cos = np.cos(angles)
    sin = np.sin(angles)
    first = np.concatenate([cos[:KEPT], -sin[1:HALF]], axis=0)
    weight = np.full(N, 2.0)
    weight[0] = weight[HALF] = 1.0
    last = -FRACTION * np.concatenate(
        [cos[:, :KEPT] * weight[None, :KEPT], -2.0 * sin[:, 1:HALF]], axis=1
    )
    forward = np.block([[cos, -sin], [sin, cos]])
    inverse = np.block([[cos, sin], [-sin, cos]])
    x = np.arange(N).reshape(4, 2, 2, 2, 4)
    order = np.concatenate([x[:, :, :, c][:, [c, 1 - c]].reshape(HALF) for c in range(2)])
    both = np.concatenate([order, order + N])
    every = (first, last, forward, inverse, forward.T[:, both], inverse.T[both, :])
    return [np.asarray(t, np.float32).astype(ml_dtypes.bfloat16) for t in every]


def coulomb_kernel():
    counter = np.arange(N)
    wrapped = np.where(counter < HALF, counter, counter - N)
    wave = (2.0 * math.pi / CELL * wrapped) ** 2
    wave_sq = wave[:KEPT, None, None] + wave[None, :, None] + wave[None, None, :]
    radius = CELL * (3.0 / (4.0 * math.pi)) ** (1.0 / 3.0)
    safe_sq = np.where(wave_sq > 0, wave_sq, 1.0)
    values = np.where(
        wave_sq > 0,
        4.0 * math.pi * (1.0 - np.cos(np.sqrt(safe_sq) * radius)) / safe_sq,
        2.0 * math.pi * radius * radius,
    )
    values = values / N**3
    values = np.concatenate([values, np.zeros((1, N, N))]).astype(np.float32)
    return values.astype(ml_dtypes.bfloat16).reshape(2, SHARE, N, N)


def dot(left, right):
    return jnp.dot(left, right, preferred_element_type=F32)


def forward_kernel(count, info, *refs):
    pieces, t_all, first, lane_fwd, mine, give = refs[: 2 * count], *refs[2 * count : 2 * count + 5]
    wide, pq, o_buf, out_sem = refs[2 * count + 5 :]
    core = info[0]
    zeros = jnp.zeros((SLAB, N), BF16)
    pq[0:SLAB, N:] = zeros
    pq[HALF * SLAB : KEPT * SLAB, N:] = zeros
    pq[KEPT * SLAB :, 0:N] = zeros
    pq[KEPT * SLAB :, N:] = zeros
    stores = []
    for i in range(count):
        t_at = [4 * info[1 + i] + 2 * core, 4 * info[1 + i] + 2 * (1 - core)]
        for j in range(0, SLAB, 2):
            density = jnp.concatenate(
                [
                    pieces[2 * i + m // 8][m % 8] * t_all[t_at[m // 8] + m // 4 % 2, m % 4]
                    for m in (j, j + 1)
                ],
                axis=1,
            )
            out = dot(first[...], density)
            wide[pl.ds(j * FIRST_PITCH, N)] = out[:, :N]
            wide[pl.ds((j + 1) * FIRST_PITCH, N)] = out[:, N:]
        for k in range(KEPT):
            rows = pl.ds(k * SLAB, SLAB)
            pq[rows, 0:N] = wide[pl.ds(k, SLAB, stride=FIRST_PITCH)].astype(BF16)
            if 0 < k < HALF:
                pq[rows, N:] = wide[pl.ds(HALF + k, SLAB, stride=FIRST_PITCH)].astype(BF16)
        for part in range(PLANES // CHUNK):
            out = dot(pq[pl.ds(part * CHUNK * SLAB, CHUNK * SLAB)], lane_fwd[...]).astype(BF16)
            half, ks = part // 3, pl.ds(part % 3 * CHUNK, CHUNK)
            o_buf[i, half, ks, 0] = out[:, :N].reshape(CHUNK, SLAB, N)
            o_buf[i, half, ks, 1] = out[:, N:].reshape(CHUNK, SLAB, N)
        stores.append(pltpu.make_async_copy(o_buf.at[i, core], mine.at[i], out_sem.at[i, 0]))
        stores.append(pltpu.make_async_copy(o_buf.at[i, 1 - core], give.at[i], out_sem.at[i, 1]))
        stores[-1].start()
        stores[-2].start()
    for copy in stores:
        copy.wait()


HBM = pl.BlockSpec(memory_space=pltpu.HBM)
VMEM = pl.BlockSpec(memory_space=pltpu.VMEM)
SMEM = pl.BlockSpec(memory_space=pltpu.SMEM)


def forward(info, pieces, t_all, consts):
    count = len(pieces) // 2
    out = jax.ShapeDtypeStruct((count, SHARE, 2, SLAB, N), BF16)
    return pl.pallas_call(
        functools.partial(forward_kernel, count),
        out_shape=(out, out),
        in_specs=[SMEM] + [VMEM] * (2 * count + 3),
        out_specs=(HBM, HBM),
        scratch_shapes=[
            pltpu.VMEM((SLAB * FIRST_PITCH, N), F32),
            pltpu.VMEM((PLANES * SLAB, 2 * N), BF16),
            pltpu.VMEM((count, 2, SHARE, 2, SLAB, N), BF16),
            pltpu.SemaphoreType.DMA((count, 2)),
        ],
        compiler_params=pltpu.CompilerParams(vmem_limit_bytes=8 * MIB),
        cost_estimate=pl.CostEstimate(
            flops=count * 3500 * 256 * 256, bytes_accessed=count << 21, transcendentals=0
        ),
        name="forward",
    )(info, *pieces, t_all, consts[0], consts[2])


STEPS = ((0, 1, 7), (2, 6), (3, 5, 4))


def middle_kernel(info, *refs):
    own, come = refs[:3], refs[3:6]
    k_hbm, row_fwd, row_inv, mine, give, spec, done, k_buf, in_sem, k_sem, out_sem = refs[6:]
    core, place = info[0], info[1]
    parts = SHARE // CHUNK

    def loads(part):
        ks = pl.ds(part * CHUNK, CHUNK)
        copies = [pltpu.make_async_copy(k_hbm.at[core, ks], k_buf.at[ks], k_sem.at[part])]
        for step, distances in enumerate(STEPS):
            for i, distance in enumerate(distances):
                at = lax.rem(place + 8 - distance, 8)
                for side, (refs_of, row) in enumerate(((own, core), (come, 1 - core))):
                    rows = pl.ds(pl.multiple_of(row * HALF + at % 4 * SLAB, SLAB), SLAB)
                    copies.append(
                        pltpu.make_async_copy(
                            refs_of[step].at[i, ks],
                            spec.at[at // 4, ks, :, rows],
                            in_sem.at[part, distance, side],
                        )
                    )
        return copies

    def stores(part):
        ks = pl.ds(part * CHUNK, CHUNK)
        copies = []
        for side, (ref, row) in enumerate(((mine, core), (give, 1 - core))):
            rows = pl.ds(pl.multiple_of(row * HALF, HALF), HALF)
            copies.append(
                pltpu.make_async_copy(
                    done.at[:, ks, :, rows], ref.at[:, ks], out_sem.at[part, side]
                )
            )
        return copies

    for part in range(parts):
        for copy in loads(part):
            copy.start()
    for part in range(parts):
        for copy in loads(part):
            copy.wait()
        for k in range(part * CHUNK, (part + 1) * CHUNK):
            both = jnp.concatenate(
                [spec[0, k].reshape(2 * N, N), spec[1, k].reshape(2 * N, N)], axis=1
            )
            out = dot(row_fwd[...], both)
            scale = jnp.concatenate([k_buf[k], k_buf[k]], axis=1).astype(F32)
            out = jnp.concatenate([out[:N] * scale, out[N:] * scale], axis=0).astype(BF16)
            out = dot(row_inv[...], out).astype(BF16)
            done[0, k] = out[:, :N].reshape(2, N, N)
            done[1, k] = out[:, N:].reshape(2, N, N)
        for copy in stores(part):
            copy.start()
    for part in range(parts):
        for copy in stores(part):
            copy.wait()


def middle(info, own, come, consts):
    out = jax.ShapeDtypeStruct((2, SHARE, 2, HALF, N), BF16)
    return pl.pallas_call(
        middle_kernel,
        out_shape=(out, out),
        in_specs=[SMEM] + [HBM] * 7 + [VMEM] * 2,
        out_specs=(HBM, HBM),
        scratch_shapes=[
            pltpu.VMEM((2, SHARE, 2, N, N), BF16),
            pltpu.VMEM((2, SHARE, 2, N, N), BF16),
            pltpu.VMEM((SHARE, N, N), BF16),
            pltpu.SemaphoreType.DMA((3, 8, 2)),
            pltpu.SemaphoreType.DMA((3,)),
            pltpu.SemaphoreType.DMA((3, 2)),
        ],
        compiler_params=pltpu.CompilerParams(vmem_limit_bytes=14 * MIB),
        cost_estimate=pl.CostEstimate(
            flops=2 * 17000 * 256 * 256, bytes_accessed=11 << 20, transcendentals=0
        ),
        name="middle",
    )(info, *own, *come, jnp.asarray(coulomb_kernel()), consts[4], consts[5])


def inverse_kernel(info, *refs):
    pieces, own, come, last, lane_inv, field = refs[:16], *refs[16:21]
    s_buf, spec, wide, f_buf, s_sem, in_sem, out_sem = refs[21:]
    core, place = info[0], info[1]
    loads = []
    for part in range(4):
        rows = pl.ds(part * SLAB, SLAB)
        loads.append(
            [
                pltpu.make_async_copy(
                    ref.at[:, :, :, rows], spec.at[part, :, half], in_sem.at[part, side]
                )
                for side, (ref, half) in enumerate(((own, core), (come, 1 - core)))
            ]
        )
    sources = []
    for distance in range(8):
        at = lax.rem(place + 8 - distance, 8)
        for i in range(2):
            sources.append(
                pltpu.make_async_copy(
                    pieces[2 * distance + i], s_buf.at[at // 4, at % 4, i], s_sem.at[distance, i]
                )
            )
    for copy in loads[0] + sources:
        copy.start()
    for copies in loads[1:]:
        for copy in copies:
            copy.start()

    def stores(part):
        return [
            pltpu.make_async_copy(
                f_buf.at[part, p], field.at[pl.ds(4 * part + 2 * bit, 2)], out_sem.at[part, p]
            )
            for p, bit in enumerate((core, 1 - core))
        ]

    for part in range(4):
        for copy in loads[part]:
            copy.wait()
        for h in range(2):
            distance = lax.rem(place + 8 - (4 * h + part), 8)
            for i in range(2):
                pltpu.make_async_copy(
                    pieces[i], s_buf.at[h, part, i], s_sem.at[distance, i]
                ).wait()

        for h in range(2):
            for chunk in range(PLANES // CHUNK):
                half, ks = chunk // 3, pl.ds(chunk % 3 * CHUNK, CHUNK)
                p = spec[part, h, half, ks, 0].reshape(CHUNK * SLAB, N)
                q = spec[part, h, half, ks, 1].reshape(CHUNK * SLAB, N)
                out = dot(jnp.concatenate([p, q], axis=1), lane_inv[...])
                base = chunk * CHUNK
                top = min(base + CHUNK, KEPT)
                wide3 = wide.reshape(N, LAST_PITCH, N)
                wide3[pl.ds(base, top - base), 0:SLAB] = out[: (top - base) * SLAB, :N].reshape(top - base, SLAB, N)
                lo, hi = max(base, 1), min(base + CHUNK, HALF)
                wide3[pl.ds(HALF + lo, hi - lo), 0:SLAB] = out[
                    (lo - base) * SLAB : (hi - base) * SLAB, N:
                ].reshape(hi - lo, SLAB, N)
            for j in range(0, SLAB, 2):
                half_spec = jnp.concatenate(
                    [wide[pl.ds(m, N, stride=LAST_PITCH)].astype(BF16) for m in (j, j + 1)], axis=1
                )
                out = dot(last[...], half_spec)
                for m in (j, j + 1):
                    term = out[:, (m - j) * N : (m - j + 1) * N] * s_buf[
                        h, part, m // 8, m % 8
                    ].astype(F32)
                    at = (part, m // 8, m // 4 % 2, m % 4)
                    if h == 1:
                        term = f_buf[at].astype(F32) + term
                    f_buf[at] = term.astype(BF16)
        for copy in stores(part):
            copy.start()
    for part in range(4):
        for copy in stores(part):
            copy.wait()


def inverse(info, pieces, own, come, consts):
    return pl.pallas_call(
        inverse_kernel,
        out_shape=jax.ShapeDtypeStruct((16, 4, N, N), BF16),
        in_specs=[SMEM] + [HBM] * 18 + [VMEM] * 2,
        out_specs=HBM,
        scratch_shapes=[
            pltpu.VMEM((2, 4, 2, SLAB // 2, N, N), BF16),
            pltpu.VMEM((4, 2, 2, SHARE, 2, SLAB, N), BF16),
            pltpu.VMEM((LAST_PITCH * N, N), F32),
            pltpu.VMEM((4, 2, 2, 4, N, N), BF16),
            pltpu.SemaphoreType.DMA((8, 2)),
            pltpu.SemaphoreType.DMA((4, 2)),
            pltpu.SemaphoreType.DMA((4, 2)),
        ],
        compiler_params=pltpu.CompilerParams(vmem_limit_bytes=16 * MIB),
        cost_estimate=pl.CostEstimate(
            flops=2 * 14000 * 256 * 256, bytes_accessed=11 << 20, transcendentals=0
        ),
        name="inverse",
    )(info, *pieces, own, come, consts[1], consts[3])


def along_z(value, by):
    return lax.ppermute(value, ("h", "l"), [(i, (i + by) % 8) for i in range(8)])


def swap_core(value):
    return lax.ppermute(value, "c", [(0, 1), (1, 0)])


TRIPS = [
    ((4 * h + l) * 2 + bit, (l + (2, 6)[bit]) % 8 * 2 + h)
    for h in range(2)
    for l in range(4)
    for bit in range(2)
]


def to_work(value):
    return lax.ppermute(value, ("h", "l", "c"), TRIPS)


def to_owner(value):
    return lax.ppermute(value, ("h", "l", "c"), [(b, a) for a, b in TRIPS])


def over_plane(value):
    return lax.all_to_all(value, ("y", "x"), 0, 0, tiled=True)


def on_device(source_bands, target_bands):
    core = lax.axis_index("c").astype(jnp.int32)
    place = (lax.axis_index("h") * 4 + lax.axis_index("l")).astype(jnp.int32)
    consts = [jnp.asarray(t) for t in tables()]

    planes = source_bands[0].reshape(2, 2, 4, N, N)
    stay = lax.dynamic_index_in_dim(planes, core, 1, keepdims=False).reshape(8, N, N)
    other = lax.dynamic_index_in_dim(planes, 1 - core, 1, keepdims=False).reshape(8, N, N)
    other = swap_core(other)

    target = to_work(target_bands[0])

    at = {0: (stay, other)}
    first = along_z(stay, 1), along_z(stay, -1)
    t_all = over_plane(jnp.broadcast_to(target[None], (16, 4, N, N)))

    at[1] = (first[0], along_z(other, 1))
    at[7] = (first[1], along_z(other, -1))
    for k in range(2, 4):
        up, down = at[k - 1], at[9 - k]
        at[k] = tuple(along_z(piece, 1) for piece in up)
        at[8 - k] = tuple(along_z(piece, -1) for piece in down)

    own, come = [], []
    for distances in STEPS:
        if 4 in distances:
            up, own[0] = lax.optimization_barrier((at[3][0], own[0]))
            last = (along_z(up, 1), along_z(at[5][1], -1))
            *at[4], own[1] = lax.optimization_barrier((*last, own[1]))
        info = jnp.stack([core] + [(place + 8 - d) % 4 for d in distances])
        mine, give = forward(info, [p for d in distances for p in at[d]], t_all, consts)
        own.append(mine)
        come.append(swap_core(give))

    info = jnp.stack([core, place])
    mine, give = middle(info, own, come, consts)
    field = inverse(info, [p for d in range(8) for p in at[d]], mine, swap_core(give), consts)
    field = jnp.sum(over_plane(field).astype(F32), axis=0).astype(BF16)
    return to_owner(field).astype(F32)[None]


def solution(mesh):
    fine = Mesh(mesh.devices.reshape(4, 4, 2, 4, 2), ("y", "x", "h", "l", "c"))
    src, tgt = ("y", "x", "h"), ("l", "c")
    return jax.shard_map(
        on_device,
        mesh=fine,
        in_specs=(P(src, tgt, None, None), P(tgt, src, None, None)),
        out_specs=P(tgt, src, None, None),
        check_vma=False,
    )
```
